32 devices in a mesh: groups: 2 (over y), tm: 4 (over x, core), gz: 4 (over z).
Axes of the slice: x: 2, y: 2, z: 4, core: 2. Of those that a mesh axis runs over, the one named last changes fastest.
Arguments:
- initial_state: float32 [32, 16, 256], P(('groups', 'gz')), parts along dimension 0, may hold values from -6 to 6
- start_guess: float32 [4, 32, 16, 256], P('tm', ('groups', 'gz')), parts along dimension 1, may hold values from -6 to 6
- control: float32 [4, 32, 16, 256], P('tm', ('groups', 'gz')), parts along dimension 1, may hold values from -6 to 6
- reaction_rate: float32 [4, 32, 16, 256], P('tm', ('groups', 'gz')), parts along dimension 1, may hold values from 0.05 to 8
Outputs:
- node_states: float32 [4, 3, 32, 16, 256], P('tm', None, ('groups', 'gz')), parts along dimension 2
The draws below stay inside these ranges and needn't reach their ends.
There are 2 independent parts, one for each index of `groups`. The reference program is written for one: setup_inputs(seed, part) draws one part's arguments, and reference() takes and returns one part's arrays. A program takes and returns all parts, laid end to end along the dimension named above; each array names one. Nothing has to cross between parts.
All inputs are finite; a program needn't handle non-finite values.
Results may differ from the reference program's by a relative error of at most 0.0001.
Values sent between devices are 32-bit elements; how exact they have to be, the bound alone decides.
A program may use at most 64 MiB of HBM per device.

```python
import math
import jax
import jax.numpy as jnp
from jax import lax

NX = 16
NY = 256
ITERS = 2
SLICES = 4
NZ = 16


def block_levels(own_key, dims, cuts, least, largest):
    def one(position, parts):
        draws = jax.random.uniform(jax.random.fold_in(jax.random.fold_in(own_key, 6), position), (parts,), jnp.float32, least / len(cuts), largest / len(cuts))
        return jnp.repeat(jnp.exp(draws), dims[position] // parts).reshape((-1,) + (1,) * (len(dims) - position - 1))

    gain = one(*cuts[0])
    for cut in cuts[1:]:
        gain = gain * one(*cut)
    return gain


def noise(own_key, extent, width, reach, shards=(), dtype=jnp.bfloat16):
    factor_of = block_levels(own_key, extent, shards, -0.22, 0.18) if shards else 1.0
    array = jax.random.normal(own_key, extent, jnp.float32) * width * factor_of
    return jnp.minimum(jnp.maximum(array, -reach), reach).astype(dtype)


def setup_inputs(seed: int = 0, part: int = 0) -> dict:
    key_of = jax.random.split(jax.random.key(seed), 5)
    part_keys = jax.random.split(jax.random.fold_in(key_of[4], part), 5)
    initial_state = noise(part_keys[0], (NZ, NX, NY), 1.0, 6.0, ((0, 4),), jnp.float32)
    start_guess = noise(part_keys[1], (SLICES, NZ, NX, NY), 1.0, 6.0, ((0, 4), (1, 4)), jnp.float32)
    control = noise(part_keys[2], (SLICES, NZ, NX, NY), 1.0, 6.0, ((0, 4), (1, 4)), jnp.float32)
    reaction_rate = jnp.clip(jnp.exp(math.log(8.0) - 5.075174 * jax.random.uniform(part_keys[3], (SLICES, NZ, NX, NY), jnp.float32) ** block_levels(part_keys[3], (SLICES, NZ, NX, NY), ((0, 4), (1, 4)), -0.2, 0.2)), 0.05, 8.0)
    return {"initial_state": initial_state, "start_guess": start_guess, "control": control, "reaction_rate": reaction_rate}


root_six = math.sqrt(6.0)
radau_matrix = (((88.0 - 7.0 * root_six) / 360.0, (296.0 - 169.0 * root_six) / 1800.0, (-2.0 + 3.0 * root_six) / 225.0), ((296.0 + 169.0 * root_six) / 1800.0, (88.0 + 7.0 * root_six) / 360.0, (-2.0 - 3.0 * root_six) / 225.0), ((16.0 - root_six) / 36.0, (16.0 + root_six) / 36.0, 1.0 / 9.0))
diffusion = 0.1

def laplace_padded(padded):
    middle = padded[..., 1:-1, :, :]
    planar = jnp.pad(middle, ((0, 0),) * (middle.ndim - 2) + ((1, 1), (1, 1)))
    summed = padded[..., 2:, :, :] + padded[..., :-2, :, :]
    summed = summed + planar[..., 2:, 1:-1] + planar[..., :-2, 1:-1]
    summed = summed + planar[..., 1:-1, 2:] + planar[..., 1:-1, :-2]
    return summed - 6.0 * middle

def pad_depth(values):
    return jnp.pad(values, ((0, 0),) * (values.ndim - 3) + ((1, 1), (0, 0), (0, 0)))

def forcing(states, laplace, control, rate):
    return diffusion * laplace + jnp.tanh(states) + control - rate * states

def integrate(values):
    return jnp.stack([radau_matrix[row_index][0] * values[0] + radau_matrix[row_index][1] * values[1] + radau_matrix[row_index][2] * values[2] for row_index in range(3)])

def restrict(values):
    shape = values.shape
    blocks = values.reshape(shape[:-2] + (shape[-2] // 2, 2, shape[-1] // 2, 2))
    return 0.25 * lax.optimization_barrier(jnp.sum(blocks, axis=(-3, -1)))

def prolong(values):
    return jnp.repeat(jnp.repeat(values, 2, axis=-2), 2, axis=-1)

def reference(initial_state, start_guess, control, reaction_rate):
    slices = start_guess.shape[0]
    diagonal = jnp.asarray([radau_matrix[index][index] for index in range(3)], jnp.float32).reshape(3, 1, 1, 1)
    node_list = [jnp.stack([start_guess[slice_index]] * 3) for slice_index in range(slices)]
    starts = [initial_state] + [start_guess[slice_index] for slice_index in range(1, slices)]
    coarse_first = restrict(initial_state)
    for number in range(ITERS):
        swept_list, scale_list, offset_list, coarse_list = ([], [], [], [])
        for slice_index in range(slices):
            states = node_list[slice_index]
            rate_here = reaction_rate[slice_index]
            control_here = control[slice_index]
            integral = integrate(forcing(states, laplace_padded(pad_depth(states)), control_here, rate_here))
            swept = (starts[slice_index] + integral + diagonal * rate_here * states) / (1.0 + diagonal * rate_here)
            fine_sum = integrate(forcing(swept, laplace_padded(pad_depth(swept)), control_here, rate_here))
            coarse = restrict(swept)
            coarse_rate = restrict(rate_here)
            coarse_scale = 1.0 / (1.0 + diagonal * coarse_rate)
            offset = coarse_scale * (restrict(fine_sum) + diagonal * coarse_rate * coarse)
            swept_list.append(swept)
            scale_list.append(coarse_scale)
            offset_list.append(offset)
            coarse_list.append(coarse)
        coarse_start = coarse_first
        for slice_index in range(slices):
            correction = scale_list[slice_index] * coarse_start + offset_list[slice_index] - coarse_list[slice_index]
            node_list[slice_index] = swept_list[slice_index] + prolong(correction)
            coarse_start = scale_list[slice_index][2] * coarse_start + offset_list[slice_index][2]
        starts = [initial_state] + [node_list[slice_index][2] for slice_index in range(slices - 1)]
    return jnp.stack(node_list)
```

```python
import functools
import math

import jax
import jax.numpy as jnp
from jax import lax
from jax.experimental import pallas as pl
from jax.experimental.pallas import tpu as pltpu
from jax.sharding import PartitionSpec as P

ITERS = 2

root_six = math.sqrt(6.0)
Q = (
    (
        (88.0 - 7.0 * root_six) / 360.0,
        (296.0 - 169.0 * root_six) / 1800.0,
        (-2.0 + 3.0 * root_six) / 225.0,
    ),
    (
        (296.0 + 169.0 * root_six) / 1800.0,
        (88.0 + 7.0 * root_six) / 360.0,
        (-2.0 - 3.0 * root_six) / 225.0,
    ),
    ((16.0 - root_six) / 36.0, (16.0 + root_six) / 36.0, 1.0 / 9.0),
)
D = tuple(Q[m][m] for m in range(3))
ROW = tuple(sum(Q[m]) for m in range(3))
diffusion = 0.1


def kernel(
    slices,
    slabs,
    init_ref,
    guess_ref,
    control_ref,
    rate_ref,
    out_ref,
    raw,
    halo_raw,
    swept_buf,
    swept_halo,
    coarse_buf,
    coarse_halo,
    corr_buf,
    corr_halo,
    end_in,
    scale_buf,
    scale_in,
    offset_buf,
    offset_in,
    out_buf,
    in_sem,
    out_sem,
    guess_send,
    guess_recv,
    swept_send,
    swept_recv,
    coarse_send,
    coarse_recv,
    corr_send,
    corr_recv,
    end_send,
    end_recv,
    scale_send,
    scale_recv,
    offset_send,
    offset_recv,
):
    t = lax.axis_index("tm")
    z = lax.axis_index("gz")
    layers, width, depth_rows = raw.shape[2], raw.shape[4], raw.shape[3]
    rows = depth_rows // 2
    has_above = z < slabs - 1
    has_below = z > 0

    sources = (guess_ref.at[0], rate_ref.at[0], control_ref.at[0], init_ref)
    loads = [
        [
            pltpu.make_async_copy(
                source.at[:, :, pl.ds(half * width, width)], raw.at[field, half], in_sem.at[field, half]
            )
            for half in range(2)
        ]
        for field, source in enumerate(sources)
    ]
    for pair in loads:
        for load in pair:
            load.start()

    @pl.when(z == 0)
    def _():
        halo_raw[0] = jnp.zeros_like(halo_raw[0])
        swept_halo[0] = jnp.zeros_like(swept_halo[0])
        corr_halo[0] = jnp.zeros_like(corr_halo[0])
        for it in range(ITERS):
            coarse_halo[it, 0] = jnp.zeros_like(coarse_halo[it, 0])

    @pl.when(z == slabs - 1)
    def _():
        halo_raw[1] = jnp.zeros_like(halo_raw[1])
        swept_halo[1] = jnp.zeros_like(swept_halo[1])
        corr_halo[1] = jnp.zeros_like(corr_halo[1])
        for it in range(ITERS):
            coarse_halo[it, 1] = jnp.zeros_like(coarse_halo[it, 1])

    barrier = pltpu.get_barrier_semaphore()

    def greet(condition, device):
        @pl.when(condition)
        def _():
            pl.semaphore_signal(barrier, inc=1, device_id=device, device_id_type=pl.DeviceIdType.MESH)

    greet(has_above, {"gz": z + 1})
    greet(has_below, {"gz": z - 1})
    for d in range(1, slices):
        greet(t >= d, {"tm": t - d})
    pl.semaphore_wait(
        barrier,
        has_above.astype(jnp.int32) + has_below.astype(jnp.int32) + (slices - 1 - t),
    )

    pending = []

    def remote(src, dst, send, recv, device, sends, receives):
        copy = pltpu.make_async_remote_copy(
            src_ref=src,
            dst_ref=dst,
            send_sem=send,
            recv_sem=recv,
            device_id=device,
            device_id_type=pl.DeviceIdType.MESH,
        )

        @pl.when(sends)
        def _():
            copy.start()

        def sent():
            @pl.when(sends)
            def _():
                copy.wait_send()

        def arrived():
            @pl.when(receives)
            def _():
                copy.wait_recv()

        pending.append(sent)
        return arrived

    def to_above(src, dst, send, recv):
        return remote(src, dst, send, recv, {"gz": z + 1}, has_above, has_below)

    def to_below(src, dst, send, recv):
        return remote(src, dst, send, recv, {"gz": z - 1}, has_below, has_above)

    def to_later(d, src, dst, send, recv):
        return remote(src, dst, send, recv, {"tm": t + d}, t + d < slices, t >= d)

    guess_arrived = []
    for half in range(2):
        columns = pl.ds(half * width, width)
        guess_arrived.append(
            to_above(
                guess_ref.at[0, layers - 1, :, columns],
                halo_raw.at[0, half],
                guess_send.at[0, half],
                guess_recv.at[0, half],
            )
        )
        guess_arrived.append(
            to_below(
                guess_ref.at[0, 0, :, columns],
                halo_raw.at[1, half],
                guess_send.at[1, half],
                guess_recv.at[1, half],
            )
        )

    lane = lax.broadcasted_iota(jnp.int32, (layers * rows, width), 1)

    def take(array, index):
        flat = array.reshape(-1, width)
        picked = jnp.take_along_axis(
            flat, index[: flat.shape[0]], axis=1, mode="promise_in_bounds"
        )
        return picked.reshape(array.shape)

    even_index = (2 * lane) % width
    odd_index = even_index + 1
    low_index = lane // 2
    high_index = low_index + width // 2
    lane3 = lax.broadcasted_iota(jnp.int32, (layers, rows, width), 2)
    row3 = lax.broadcasted_iota(jnp.int32, (layers, rows, width), 1)

    def split(low, high):
        front = lane3[: low.shape[0]] < width // 2
        return [
            jnp.where(front, take(low, index), take(high, index))
            for index in (even_index, odd_index)
        ]

    def parities(ref):
        out = []
        for px in range(2):
            low = ref[0, :, pl.ds(px, rows, stride=2), :]
            high = ref[1, :, pl.ds(px, rows, stride=2), :]
            out += split(low, high)
        return out

    def halo_parities(side):
        out = []
        for px in range(2):
            low = halo_raw[side, 0, pl.ds(px, rows, stride=2), :]
            high = halo_raw[side, 1, pl.ds(px, rows, stride=2), :]
            out += split(low[None], high[None])
        return out

    def down(v):
        return jnp.where(row3 == 0, 0.0, pltpu.roll(v, 1, 1))

    def up(v):
        return jnp.where(row3 == rows - 1, 0.0, pltpu.roll(v, rows - 1, 1))

    def right(v):
        return jnp.where(lane3 == 0, 0.0, pltpu.roll(v, 1, 2))

    def left(v):
        return jnp.where(lane3 == width - 1, 0.0, pltpu.roll(v, width - 1, 2))

    def planar(v):
        a, b, c, d = v
        return [
            (c + down(c)) + (b + right(b)),
            (d + down(d)) + (a + left(a)),
            (a + up(a)) + (d + right(d)),
            (b + up(b)) + (c + left(c)),
        ]

    def inner(v):
        below = jnp.concatenate([jnp.zeros_like(v[:1]), v[:-1]], 0)
        above = jnp.concatenate([v[1:], jnp.zeros_like(v[:1])], 0)
        return below + above

    def outer(low, high):
        gap = jnp.zeros((layers - 2, rows, width), jnp.float32)
        return jnp.concatenate([low, gap, high], 0)

    def total(v):
        return (v[0] + v[1]) + (v[2] + v[3])

    for load in loads[0]:
        load.wait()
    guess = parities(raw.at[0])
    for load in loads[1]:
        load.wait()
    rate = parities(raw.at[1])
    coarse_rate = 0.25 * total(rate)
    scale = [1.0 / (1.0 + D[m] * coarse_rate) for m in range(3)]
    scale_buf[...] = scale[2]
    scale_arrived = {
        d: to_later(d, scale_buf, scale_in.at[d - 1], scale_send.at[d - 1], scale_recv.at[d - 1])
        for d in range(1, slices)
    }
    for load in loads[2]:
        load.wait()
    control = parities(raw.at[2])
    for load in loads[3]:
        load.wait()
    initial = parities(raw.at[3])
    coarse_first = 0.25 * total(initial)
    coarse_control = 0.25 * total(control)
    leading = t == 0
    start = [jnp.where(leading, initial[p], guess[p]) for p in range(4)]
    inverse = [[1.0 / (1.0 + D[m] * rate[p]) for p in range(4)] for m in range(3)]

    def force_inside(v):
        flat = planar(v)
        return [
            diffusion * (flat[p] + inner(v[p]) - 6.0 * v[p])
            + jnp.tanh(v[p])
            + control[p]
            - rate[p] * v[p]
            for p in range(4)
        ]

    force = force_inside(guess)
    for arrived in guess_arrived:
        arrived()
    low, high = halo_parities(0), halo_parities(1)
    force = [force[p] + diffusion * outer(low[p], high[p]) for p in range(4)]
    swept = [
        [
            (start[p] + ROW[m] * force[p] + D[m] * rate[p] * guess[p]) * inverse[m][p]
            for p in range(4)
        ]
        for m in range(3)
    ]

    for it in range(ITERS):
        coarse = [0.25 * total(swept[m]) for m in range(3)]
        for m in range(3):
            coarse_buf[it, :, m] = coarse[m]
        coarse_arrived = [
            to_above(
                coarse_buf.at[it, layers - 1],
                coarse_halo.at[it, 0],
                coarse_send.at[it, 0],
                coarse_recv.at[it, 0],
            ),
            to_below(
                coarse_buf.at[it, 0],
                coarse_halo.at[it, 1],
                coarse_send.at[it, 1],
                coarse_recv.at[it, 1],
            ),
        ]
        if it + 1 < ITERS:
            for m in range(3):
                for p in range(4):
                    swept_buf[:, m, p] = swept[m][p]
            end_arrived = to_later(1, swept_buf.at[:, 2], end_in, end_send, end_recv)
            swept_arrived = [
                to_above(
                    swept_buf.at[layers - 1], swept_halo.at[0], swept_send.at[0], swept_recv.at[0]
                ),
                to_below(swept_buf.at[0], swept_halo.at[1], swept_send.at[1], swept_recv.at[1]),
            ]
        restricted = []
        for j in range(3):
            a, b, c, d = swept[j]
            edges = (down(c + d) + up(a + b)) + (right(b + d) + left(a + c))
            local = [jnp.tanh(swept[j][p]) - rate[p] * swept[j][p] for p in range(4)]
            restricted.append(
                0.25 * (diffusion * edges + total(local))
                + diffusion * (inner(coarse[j]) - 4.0 * coarse[j])
                + coarse_control
            )
        for arrived in coarse_arrived:
            arrived()
        restricted = [
            restricted[j]
            + diffusion * outer(coarse_halo[it, 0, j][None], coarse_halo[it, 1, j][None])
            for j in range(3)
        ]

        def offset_of(m):
            mixed = Q[m][0] * restricted[0] + Q[m][1] * restricted[1] + Q[m][2] * restricted[2]
            return scale[m] * (mixed + D[m] * coarse_rate * coarse[m])

        last = offset_of(2)
        offset_buf[it] = last
        offset_arrived = {
            d: to_later(
                d,
                offset_buf.at[it],
                offset_in.at[it, d - 1],
                offset_send.at[it, d - 1],
                offset_recv.at[it, d - 1],
            )
            for d in reversed(range(1, slices))
        }
        offset = [offset_of(0), offset_of(1), last]
        if it == 0:
            for d in range(1, slices):
                scale_arrived[d]()
        for d in range(1, slices):
            offset_arrived[d]()
        coarse_start = coarse_first
        for d in reversed(range(1, slices)):
            coarse_start = jnp.where(
                t >= d, scale_in[d - 1] * coarse_start + offset_in[it, d - 1], coarse_start
            )
        correction = [scale[m] * coarse_start + offset[m] - coarse[m] for m in range(3)]
        if it + 1 == ITERS:
            break
        for m in range(3):
            corr_buf[:, m] = correction[m]
        corr_arrived = [
            to_above(corr_buf.at[layers - 1], corr_halo.at[0], corr_send.at[0], corr_recv.at[0]),
            to_below(corr_buf.at[0], corr_halo.at[1], corr_send.at[1], corr_recv.at[1]),
        ]
        nodes = [[swept[m][p] + correction[m] for p in range(4)] for m in range(3)]
        forces = [force_inside(nodes[j]) for j in range(3)]
        end_arrived()
        ends = [end_in[:, p] for p in range(4)]
        shift = coarse_start - 0.25 * total(ends)
        start = [jnp.where(leading, initial[p], ends[p] + shift) for p in range(4)]
        for arrived in swept_arrived + corr_arrived:
            arrived()
        for j in range(3):
            for p in range(4):
                low = (swept_halo[0, j, p] + corr_halo[0, j])[None]
                high = (swept_halo[1, j, p] + corr_halo[1, j])[None]
                forces[j][p] = forces[j][p] + diffusion * outer(low, high)
        swept = [
            [
                (
                    start[p]
                    + (Q[m][0] * forces[0][p] + Q[m][1] * forces[1][p] + Q[m][2] * forces[2][p])
                    + D[m] * rate[p] * nodes[m][p]
                )
                * inverse[m][p]
                for p in range(4)
            ]
            for m in range(3)
        ]

    even_lane = lane3 % 2 == 0
    stores = []
    for m in range(3):
        node = [swept[m][p] + correction[m] for p in range(4)]
        for half, index in enumerate((low_index, high_index)):
            for px in range(2):
                out_buf[m, half, :, pl.ds(px, rows, stride=2), :] = jnp.where(
                    even_lane, take(node[2 * px], index), take(node[2 * px + 1], index)
                )
            store = pltpu.make_async_copy(
                out_buf.at[m, half],
                out_ref.at[0, m, :, :, pl.ds(half * width, width)],
                out_sem.at[m, half],
            )
            store.start()
            stores.append(store)
    for sent in pending:
        sent()
    for store in stores:
        store.wait()


def per_device(initial_state, start_guess, control, reaction_rate):
    slices = lax.axis_size("tm")
    slabs = lax.axis_size("gz")
    layers, depth_rows, columns = initial_state.shape
    rows, width = depth_rows // 2, columns // 2
    later = max(slices - 1, 1)
    vmem, dma = pltpu.VMEM, pltpu.SemaphoreType.DMA
    f32 = jnp.float32
    anywhere = pl.BlockSpec(memory_space=pl.ANY)
    return pl.pallas_call(
        functools.partial(kernel, slices, slabs),
        out_shape=jax.ShapeDtypeStruct((1, 3, layers, depth_rows, columns), f32),
        in_specs=[anywhere] * 4,
        out_specs=anywhere,
        scratch_shapes=[
            vmem((4, 2, layers, depth_rows, width), f32),
            vmem((2, 2, depth_rows, width), f32),
            vmem((layers, 3, 4, rows, width), f32),
            vmem((2, 3, 4, rows, width), f32),
            vmem((ITERS, layers, 3, rows, width), f32),
            vmem((ITERS, 2, 3, rows, width), f32),
            vmem((layers, 3, rows, width), f32),
            vmem((2, 3, rows, width), f32),
            vmem((layers, 4, rows, width), f32),
            vmem((layers, rows, width), f32),
            vmem((later, layers, rows, width), f32),
            vmem((ITERS, layers, rows, width), f32),
            vmem((ITERS, later, layers, rows, width), f32),
            vmem((3, 2, layers, depth_rows, width), f32),
            dma((4, 2)),
            dma((3, 2)),
            dma((2, 2)),
            dma((2, 2)),
            dma((2,)),
            dma((2,)),
            dma((ITERS, 2)),
            dma((ITERS, 2)),
            dma((2,)),
            dma((2,)),
            dma,
            dma,
            dma((later,)),
            dma((later,)),
            dma((ITERS, later)),
            dma((ITERS, later)),
        ],
        compiler_params=pltpu.CompilerParams(
            collective_id=0, has_side_effects=True, vmem_limit_bytes=32 * 1024 * 1024
        ),
    )(initial_state, start_guess, control, reaction_rate)


def solution(mesh):
    in_specs = (
        P(("groups", "gz"), None, None),
        P("tm", ("groups", "gz"), None, None),
        P("tm", ("groups", "gz"), None, None),
        P("tm", ("groups", "gz"), None, None),
    )
    out_specs = P("tm", None, ("groups", "gz"), None, None)
    return jax.shard_map(
        per_device, mesh=mesh, in_specs=in_specs, out_specs=out_specs, check_vma=False
    )
```

```python
import functools
import math
import types

import jax
import jax.numpy as jnp
from jax import lax
from jax.experimental import pallas as pl
from jax.experimental.pallas import tpu as pltpu
from jax.sharding import PartitionSpec as P

ITERS = 2

root_six = math.sqrt(6.0)
Q = (
    (
        (88.0 - 7.0 * root_six) / 360.0,
        (296.0 - 169.0 * root_six) / 1800.0,
        (-2.0 + 3.0 * root_six) / 225.0,
    ),
    (
        (296.0 + 169.0 * root_six) / 1800.0,
        (88.0 + 7.0 * root_six) / 360.0,
        (-2.0 - 3.0 * root_six) / 225.0,
    ),
    ((16.0 - root_six) / 36.0, (16.0 + root_six) / 36.0, 1.0 / 9.0),
)
D = tuple(Q[m][m] for m in range(3))
ROW = tuple(sum(Q[m]) for m in range(3))
diffusion = 0.1
VMEM_LIMIT = 60 * 1024 * 1024
MESH = pl.DeviceIdType.MESH


def kernel(slices, slabs, init_ref, guess_ref, control_ref, rate_ref, out_ref, r):
    t = lax.axis_index("tm")
    z = lax.axis_index("gz")
    layers, depth_rows, width = r.raw.shape[2:]
    rows = depth_rows // 2
    has_above = z < slabs - 1
    has_below = z > 0
    leading = t == 0

    sources = (guess_ref.at[0], rate_ref.at[0], control_ref.at[0], init_ref)
    halves = [pl.ds(half * width, width) for half in range(2)]
    loads = [
        [
            pltpu.make_async_copy(
                source.at[:, :, halves[half]], r.raw.at[field, half], r.in_sem.at[field, half]
            )
            for half in range(2)
        ]
        for field, source in enumerate(sources)
    ]
    for pair in loads:
        for load in pair:
            load.start()

    barrier = pltpu.get_barrier_semaphore()

    def greet(condition, device):
        @pl.when(condition)
        def _():
            pl.semaphore_signal(barrier, inc=1, device_id=device, device_id_type=MESH)

    greet(has_above, {"gz": z + 1})
    greet(has_below, {"gz": z - 1})
    for d in range(1, slices):
        greet(t >= d, {"tm": t - d})
        greet((t >= d) & has_above, {"tm": t - d, "gz": z + 1})
        greet((t >= d) & has_below, {"tm": t - d, "gz": z - 1})
    beside = has_above.astype(jnp.int32) + has_below.astype(jnp.int32)

    @pl.when(z == 0)
    def _():
        r.halo[:, :, 0] = jnp.zeros_like(r.halo[:, :, 0])

    @pl.when(z == slabs - 1)
    def _():
        r.halo[:, :, 1] = jnp.zeros_like(r.halo[:, :, 1])

    pl.semaphore_wait(barrier, beside + (slices - 1 - t) * (1 + beside))

    pending = []

    def remote(src, dst, send, recv, device, sends, receives):
        copy = pltpu.make_async_remote_copy(
            src_ref=src,
            dst_ref=dst,
            send_sem=send,
            recv_sem=recv,
            device_id=device,
            device_id_type=MESH,
        )

        @pl.when(sends)
        def _():
            copy.start()

        def sent():
            @pl.when(sends)
            def _():
                copy.wait_send()

        def arrived():
            @pl.when(receives)
            def _():
                copy.wait_recv()

        pending.append(sent)
        return arrived

    def beside_copies(sources, dst, send, recv, d=0, only=None):
        sends = t + d < slices
        receives = t >= d
        if only is not None:
            sends, receives = only
        return [
            remote(
                sources[side],
                dst(side),
                send.at[side],
                recv.at[side],
                {"tm": t + d, "gz": z + step},
                sends & here,
                receives & there,
            )
            for side, step, here, there in (
                (0, 1, has_above, has_below),
                (1, -1, has_below, has_above),
            )
        ]

    def later_copy(d, src, dst, send, recv, only=None):
        sends, receives = (t + d < slices, t >= d) if only is None else only
        return remote(src, dst, send, recv, {"tm": t + d}, sends, receives)

    always = (t >= 0, t >= 0)
    first_only = (leading, leading)

    def halo_copies(field, source, low_ring, high_ring, index, only):
        count = high_ring - low_ring + 1
        out = []
        for half in range(2):
            up = source.at[pl.ds(layers - high_ring, count), :, halves[half]]
            down = source.at[pl.ds(low_ring - 1, count), :, halves[half]]
            starts = (3 - high_ring, low_ring - 1)
            out += beside_copies(
                (up, down),
                lambda side: r.halo.at[field, half, side, pl.ds(starts[side], count)],
                r.halo_send.at[index, half],
                r.halo_recv.at[index, half],
                only=only,
            )
        return out

    guess_src, rate_src, control_src, init_src = sources
    near = halo_copies(0, guess_src, 1, 2, 0, always)
    near += halo_copies(1, rate_src, 1, 1, 1, always)
    near += halo_copies(2, control_src, 1, 1, 2, always)
    near += halo_copies(3, init_src, 1, 1, 3, first_only)
    far = halo_copies(1, rate_src, 2, 2, 4, always)
    far += halo_copies(0, guess_src, 3, 3, 5, always)
    far += halo_copies(2, control_src, 2, 2, 6, always)
    far += halo_copies(3, init_src, 2, 2, 7, first_only)

    lane = lax.broadcasted_iota(jnp.int32, (layers * rows, width), 1)
    lane3 = lax.broadcasted_iota(jnp.int32, (layers, rows, width), 2)
    row3 = lax.broadcasted_iota(jnp.int32, (layers, rows, width), 1)
    even_index = (2 * lane) % width
    odd_index = even_index + 1
    low_index = lane // 2
    high_index = low_index + width // 2

    def take(array, index):
        flat = array.reshape(-1, width)
        picked = jnp.take_along_axis(
            flat, index[: flat.shape[0]], axis=1, mode="promise_in_bounds"
        )
        return picked.reshape(array.shape)

    def split(low, high):
        front = lane3[: low.shape[0]] < width // 2
        return [
            jnp.where(front, take(low, index), take(high, index))
            for index in (even_index, odd_index)
        ]

    def core_of(field):
        for load in loads[field]:
            load.wait()
        out = []
        for px in range(2):
            low = r.raw[field, 0, :, pl.ds(px, rows, stride=2), :]
            high = r.raw[field, 1, :, pl.ds(px, rows, stride=2), :]
            out += split(low, high)
        return out

    def rim_of(field, ring):
        out = []
        for px in range(2):
            low, high = [
                jnp.concatenate(
                    [
                        r.halo[field, half, side, index, pl.ds(px, rows, stride=2), :][None]
                        for side, index in ((0, 3 - ring), (1, ring - 1))
                    ],
                    0,
                )
                for half in range(2)
            ]
            out += split(low, high)
        return out

    rim_side = lax.broadcasted_iota(jnp.int32, (2, rows, width), 0)
    rim_inside = ((rim_side == 0) & has_below) | ((rim_side == 1) & has_above)

    def inside(v):
        return jnp.where(rim_inside, v, 0.0)

    def down(v):
        return jnp.where(row3[: v.shape[0]] == 0, 0.0, pltpu.roll(v, 1, 1))

    def up(v):
        return jnp.where(row3[: v.shape[0]] == rows - 1, 0.0, pltpu.roll(v, rows - 1, 1))

    def right(v):
        return jnp.where(lane3[: v.shape[0]] == 0, 0.0, pltpu.roll(v, 1, 2))

    def left(v):
        return jnp.where(lane3[: v.shape[0]] == width - 1, 0.0, pltpu.roll(v, width - 1, 2))

    def planar(v):
        a, b, c, d = v
        return [
            (c + down(c)) + (b + right(b)),
            (d + down(d)) + (a + left(a)),
            (a + up(a)) + (d + right(d)),
            (b + up(b)) + (c + left(c)),
        ]

    def inner(v):
        below = jnp.concatenate([jnp.zeros_like(v[:1]), v[:-1]], 0)
        above = jnp.concatenate([v[1:], jnp.zeros_like(v[:1])], 0)
        return below + above

    def outer(rim):
        gap = jnp.zeros((layers - 2, rows, width), jnp.float32)
        return jnp.concatenate([rim[:1], gap, rim[1:]], 0)

    def ends_of(v):
        return jnp.concatenate([v[:1], v[layers - 1 :]], 0)

    def total(v):
        return (v[0] + v[1]) + (v[2] + v[3])

    def force_of(v, depth, control, rate):
        flat = planar(v)
        return [
            diffusion * (flat[p] + depth[p] - 6.0 * v[p])
            + jnp.tanh(v[p])
            + control[p]
            - rate[p] * v[p]
            for p in range(4)
        ]

    def sweep_of(start, integral, rate, nodes, inverse):
        return [
            [
                (start[p] + integral[m][p] + D[m] * rate[p] * nodes[m][p]) * inverse[m][p]
                for p in range(4)
            ]
            for m in range(3)
        ]

    def inverse_of(rate):
        return [[1.0 / (1.0 + D[m] * rate[p]) for p in range(4)] for m in range(3)]

    def scale_of(coarse_rate):
        return [1.0 / (1.0 + D[m] * coarse_rate) for m in range(3)]

    def first_sweep(start, force, rate, guess, inverse):
        integral = [[ROW[m] * force[p] for p in range(4)] for m in range(3)]
        return sweep_of(start, integral, rate, [guess] * 3, inverse)

    def mix(m, v):
        return Q[m][0] * v[0] + Q[m][1] * v[1] + Q[m][2] * v[2]

    guess = core_of(0)
    rate = core_of(1)
    coarse_rate = 0.25 * total(rate)
    scale = scale_of(coarse_rate)
    r.scale_buf[...] = scale[2]
    scale_arrived = []
    for d in range(1, slices):
        only = ((t > 0) & (t + d < slices), t > d)
        scale_arrived.append(
            later_copy(
                d,
                r.scale_buf,
                r.scale_in.at[d - 1],
                r.scale_send.at[d - 1],
                r.scale_recv.at[d - 1],
                only,
            )
        )
        scale_arrived += beside_copies(
            (r.scale_buf.at[pl.ds(layers - 2, 2)], r.scale_buf.at[pl.ds(0, 2)]),
            lambda side: r.scale_rim_in.at[d - 1, side],
            r.scale_rim_send.at[d - 1],
            r.scale_rim_recv.at[d - 1],
            d,
            only,
        )
    control = core_of(2)
    initial = core_of(3)
    coarse_first = 0.25 * total(initial)
    coarse_control = 0.25 * total(control)
    start = [jnp.where(leading, initial[p], guess[p]) for p in range(4)]
    inverse = inverse_of(rate)

    force = force_of(guess, [inner(v) for v in guess], control, rate)
    for arrived in near:
        arrived()
    guess1, guess2 = rim_of(0, 1), rim_of(0, 2)
    rate1, control1, initial1 = rim_of(1, 1), rim_of(2, 1), rim_of(3, 1)
    force = [force[p] + diffusion * outer(guess1[p]) for p in range(4)]
    swept = first_sweep(start, force, rate, guess, inverse)
    inverse1 = inverse_of(rate1)
    start1 = [jnp.where(leading, initial1[p], guess1[p]) for p in range(4)]
    force1 = force_of(guess1, [guess2[p] + ends_of(guess[p]) for p in range(4)], control1, rate1)
    swept1 = first_sweep(start1, force1, rate1, guess1, inverse1)
    swept1 = [[inside(v) for v in node] for node in swept1]

    def offsets_of(swept, coarse, coarse_rim):
        restricted = []
        for j in range(3):
            a, b, c, d = swept[j]
            edges = (down(c + d) + up(a + b)) + (right(b + d) + left(a + c))
            local = [jnp.tanh(swept[j][p]) - rate[p] * swept[j][p] for p in range(4)]
            restricted.append(
                0.25 * (diffusion * edges + total(local))
                + diffusion * (inner(coarse[j]) - 4.0 * coarse[j] + outer(coarse_rim[j]))
                + coarse_control
            )
        return [
            scale[m] * (mix(m, restricted) + D[m] * coarse_rate * coarse[m]) for m in (0, 1, 2)
        ]

    def send_offset(it, last):
        r.offset_buf[it] = jnp.where(leading, scale[2] * coarse_first + last, last)
        return [
            later_copy(
                d,
                r.offset_buf.at[it],
                r.offset_in.at[it, d - 1],
                r.offset_send.at[it, d - 1],
                r.offset_recv.at[it, d - 1],
            )
            for d in reversed(range(1, slices))
        ]

    def chain(first, scales, offsets):
        current = first
        for d in reversed(range(1, slices)):
            moved = scales(d) * current + offsets(d)
            current = jnp.where(t > d, moved, jnp.where(t == d, offsets(d), current))
        return current

    coarse = [0.25 * total(swept[m]) for m in range(3)]
    coarse1 = [0.25 * total(swept1[m]) for m in range(3)]
    offset = offsets_of(swept, coarse, coarse1)
    offset_arrived = send_offset(0, offset[2])
    for d in range(1, slices):
        offset_arrived += beside_copies(
            (r.offset_buf.at[0, pl.ds(layers - 2, 2)], r.offset_buf.at[0, pl.ds(0, 2)]),
            lambda side: r.offset_rim_in.at[d - 1, side],
            r.offset_rim_send.at[d - 1],
            r.offset_rim_recv.at[d - 1],
            d,
        )
    for m in range(3):
        r.own_buf[:, m] = offset[m]
    own_arrived = beside_copies(
        (r.own_buf.at[pl.ds(layers - 2, 2)], r.own_buf.at[pl.ds(0, 2)]),
        lambda side: r.own_rim.at[side],
        r.own_send,
        r.own_recv,
    )
    for p in range(4):
        r.end_buf[pl.ds(1, layers), p] = swept[2][p]
        r.end_buf[0, p] = swept1[2][p][0]
        r.end_buf[layers + 1, p] = swept1[2][p][1]
    end_arrived = later_copy(1, r.end_buf, r.end_in, r.end_send, r.end_recv)

    for arrived in far:
        arrived()
    guess3 = rim_of(0, 3)
    rate2, control2, initial2 = rim_of(1, 2), rim_of(2, 2), rim_of(3, 2)
    start2 = [jnp.where(leading, initial2[p], guess2[p]) for p in range(4)]
    force2 = force_of(guess2, [guess3[p] + guess1[p] for p in range(4)], control2, rate2)
    swept2 = first_sweep(start2, force2, rate2, guess2, inverse_of(rate2))
    coarse2 = [0.25 * total(swept2[m]) for m in range(3)]
    scale1, scale2 = scale_of(0.25 * total(rate1)), scale_of(0.25 * total(rate2))

    for arrived in scale_arrived + offset_arrived:
        arrived()
    coarse_start = chain(
        coarse_first, lambda d: r.scale_in[d - 1], lambda d: r.offset_in[0, d - 1]
    )

    def ring(ref, k):
        return jnp.concatenate([ref[0, 2 - k][None], ref[1, k - 1][None]], 0)

    start_rim = [
        chain(
            0.25 * total(initial_ring),
            lambda d: ring(r.scale_rim_in.at[d - 1], k),
            lambda d: ring(r.offset_rim_in.at[d - 1], k),
        )
        for k, initial_ring in ((1, initial1), (2, initial2))
    ]
    correction = [scale[m] * coarse_start + offset[m] - coarse[m] for m in range(3)]
    nodes = [[swept[m][p] + correction[m] for p in range(4)] for m in range(3)]
    for arrived in own_arrived:
        arrived()

    def rim_nodes(k, scales, coarses, sweeps):
        own = ring(r.own_rim, k)
        out = []
        for m in range(3):
            corrected = scales[m] * start_rim[k - 1] + own[:, m] - coarses[m]
            out.append([inside(sweeps[m][p] + corrected) for p in range(4)])
        return out

    nodes1 = rim_nodes(1, scale1, coarse1, swept1)
    nodes2 = rim_nodes(2, scale2, coarse2, swept2)
    forces = [
        force_of(
            nodes[j], [inner(nodes[j][p]) + outer(nodes1[j][p]) for p in range(4)], control, rate
        )
        for j in range(3)
    ]
    forces1 = [
        force_of(
            nodes1[j],
            [nodes2[j][p] + ends_of(nodes[j][p]) for p in range(4)],
            control1,
            rate1,
        )
        for j in range(3)
    ]
    integral = [[mix(m, [forces[j][p] for j in range(3)]) for p in range(4)] for m in range(3)]
    integral1 = [[mix(m, [forces1[j][p] for j in range(3)]) for p in range(4)] for m in range(3)]
    end_arrived()
    ends = [r.end_in[pl.ds(1, layers), p] for p in range(4)]
    ends1 = [
        jnp.concatenate([r.end_in[0, p][None], r.end_in[layers + 1, p][None]], 0) for p in range(4)
    ]
    shift = coarse_start - 0.25 * total(ends)
    shift1 = start_rim[0] - 0.25 * total(ends1)
    start = [jnp.where(leading, initial[p], ends[p] + shift) for p in range(4)]
    start1 = [jnp.where(leading, initial1[p], ends1[p] + shift1) for p in range(4)]
    swept = sweep_of(start, integral, rate, nodes, inverse)
    swept1 = sweep_of(start1, integral1, rate1, nodes1, inverse1)

    coarse = [0.25 * total(swept[m]) for m in range(3)]
    coarse1 = [inside(0.25 * total(swept1[m])) for m in range(3)]
    offset = offsets_of(swept, coarse, coarse1)
    for arrived in send_offset(1, offset[2]):
        arrived()
    coarse_start = chain(
        coarse_first, lambda d: r.scale_in[d - 1], lambda d: r.offset_in[1, d - 1]
    )
    correction = [scale[m] * coarse_start + offset[m] - coarse[m] for m in range(3)]

    even_lane = lane3 % 2 == 0
    stores = []
    for m in range(3):
        node = [swept[m][p] + correction[m] for p in range(4)]
        for half, index in enumerate((low_index, high_index)):
            for px in range(2):
                r.out_buf[m, half, :, pl.ds(px, rows, stride=2), :] = jnp.where(
                    even_lane, take(node[2 * px], index), take(node[2 * px + 1], index)
                )
            store = pltpu.make_async_copy(
                r.out_buf.at[m, half],
                out_ref.at[0, m, :, :, halves[half]],
                r.out_sem.at[m, half],
            )
            store.start()
            stores.append(store)
    for sent in pending:
        sent()
    for store in stores:
        store.wait()


def per_device(initial_state, start_guess, control, reaction_rate):
    slices = lax.axis_size("tm")
    slabs = lax.axis_size("gz")
    layers, depth_rows, columns = initial_state.shape
    rows, width = depth_rows // 2, columns // 2
    later = slices - 1
    vmem = functools.partial(pltpu.VMEM, dtype=jnp.float32)
    dma = pltpu.SemaphoreType.DMA
    coarse = (layers, rows, width)
    scratch = dict(
        raw=vmem((4, 2, layers, depth_rows, width)),
        halo=vmem((4, 2, 2, 3, depth_rows, width)),
        scale_buf=vmem(coarse),
        scale_in=vmem((later,) + coarse),
        scale_rim_in=vmem((later, 2, 2, rows, width)),
        offset_buf=vmem((ITERS,) + coarse),
        offset_in=vmem((ITERS, later) + coarse),
        offset_rim_in=vmem((later, 2, 2, rows, width)),
        own_buf=vmem((layers, 3, rows, width)),
        own_rim=vmem((2, 2, 3, rows, width)),
        end_buf=vmem((layers + 2, 4, rows, width)),
        end_in=vmem((layers + 2, 4, rows, width)),
        out_buf=vmem((3, 2, layers, depth_rows, width)),
        in_sem=dma((4, 2)),
        out_sem=dma((3, 2)),
        halo_send=dma((8, 2, 2)),
        halo_recv=dma((8, 2, 2)),
        scale_send=dma((later,)),
        scale_recv=dma((later,)),
        scale_rim_send=dma((later, 2)),
        scale_rim_recv=dma((later, 2)),
        offset_send=dma((ITERS, later)),
        offset_recv=dma((ITERS, later)),
        offset_rim_send=dma((later, 2)),
        offset_rim_recv=dma((later, 2)),
        own_send=dma((2,)),
        own_recv=dma((2,)),
        end_send=dma,
        end_recv=dma,
    )
    names = list(scratch)

    def body(*refs):
        kernel(slices, slabs, *refs[:5], types.SimpleNamespace(**dict(zip(names, refs[5:]))))

    return pl.pallas_call(
        body,
        out_shape=jax.ShapeDtypeStruct((1, 3, layers, depth_rows, columns), jnp.float32),
        in_specs=[pl.BlockSpec(memory_space=pl.ANY)] * 4,
        out_specs=pl.BlockSpec(memory_space=pl.ANY),
        scratch_shapes=list(scratch.values()),
        compiler_params=pltpu.CompilerParams(
            collective_id=0, has_side_effects=True, vmem_limit_bytes=VMEM_LIMIT
        ),
    )(initial_state, start_guess, control, reaction_rate)


def solution(mesh):
    in_specs = (
        P(("groups", "gz"), None, None),
        P("tm", ("groups", "gz"), None, None),
        P("tm", ("groups", "gz"), None, None),
        P("tm", ("groups", "gz"), None, None),
    )
    out_specs = P("tm", None, ("groups", "gz"), None, None)
    return jax.shard_map(
        per_device, mesh=mesh, in_specs=in_specs, out_specs=out_specs, check_vma=False
    )
```

```python
import functools
import math
import types

import jax
import jax.numpy as jnp
from jax import lax
from jax.experimental import pallas as pl
from jax.experimental.pallas import tpu as pltpu
from jax.sharding import PartitionSpec as P

ITERS = 2

root_six = math.sqrt(6.0)
Q = (
    (
        (88.0 - 7.0 * root_six) / 360.0,
        (296.0 - 169.0 * root_six) / 1800.0,
        (-2.0 + 3.0 * root_six) / 225.0,
    ),
    (
        (296.0 + 169.0 * root_six) / 1800.0,
        (88.0 + 7.0 * root_six) / 360.0,
        (-2.0 - 3.0 * root_six) / 225.0,
    ),
    ((16.0 - root_six) / 36.0, (16.0 + root_six) / 36.0, 1.0 / 9.0),
)
D = tuple(Q[m][m] for m in range(3))
ROW = tuple(sum(Q[m]) for m in range(3))
diffusion = 0.1
VMEM_LIMIT = 60 * 1024 * 1024
MESH = pl.DeviceIdType.MESH


def kernel(slices, slabs, init_ref, guess_ref, control_ref, rate_ref, out_ref, r):
    t = lax.axis_index("tm")
    z = lax.axis_index("gz")
    layers, depth_rows, width = r.raw.shape[2:]
    rows = depth_rows // 2
    has_above = z < slabs - 1
    has_below = z > 0
    leading = t == 0

    sources = (guess_ref.at[0], rate_ref.at[0], control_ref.at[0], init_ref)
    halves = [pl.ds(half * width, width) for half in range(2)]
    loads = [
        [
            pltpu.make_async_copy(
                source.at[:, :, halves[half]], r.raw.at[field, half], r.in_sem.at[field, half]
            )
            for half in range(2)
        ]
        for field, source in enumerate(sources)
    ]
    for pair in loads:
        for load in pair:
            load.start()

    barrier = pltpu.get_barrier_semaphore()

    def greet(condition, device):
        @pl.when(condition)
        def _():
            pl.semaphore_signal(barrier, inc=1, device_id=device, device_id_type=MESH)

    greet(has_above, {"gz": z + 1})
    greet(has_below, {"gz": z - 1})
    for d in range(1, slices):
        greet(t >= d, {"tm": t - d})
        greet((t >= d) & has_above, {"tm": t - d, "gz": z + 1})
        greet((t >= d) & has_below, {"tm": t - d, "gz": z - 1})
    beside = has_above.astype(jnp.int32) + has_below.astype(jnp.int32)

    @pl.when(z == 0)
    def _():
        r.halo[:, 0] = jnp.zeros_like(r.halo[:, 0])

    @pl.when(z == slabs - 1)
    def _():
        r.halo[:, 1] = jnp.zeros_like(r.halo[:, 1])

    pl.semaphore_wait(barrier, beside + (slices - 1 - t) * (1 + beside))

    pending = []

    def remote(src, dst, send, recv, device, sends, receives):
        copy = pltpu.make_async_remote_copy(
            src_ref=src,
            dst_ref=dst,
            send_sem=send,
            recv_sem=recv,
            device_id=device,
            device_id_type=MESH,
        )

        @pl.when(sends)
        def _():
            copy.start()

        def sent():
            @pl.when(sends)
            def _():
                copy.wait_send()

        def arrived():
            @pl.when(receives)
            def _():
                copy.wait_recv()

        pending.append(sent)
        return arrived

    def beside_copies(sources, dst, send, recv, d=0, only=None):
        sends = t + d < slices
        receives = t >= d
        if only is not None:
            sends, receives = only
        return [
            remote(
                sources[side],
                dst(side),
                send.at[side],
                recv.at[side],
                {"tm": t + d, "gz": z + step},
                sends & here,
                receives & there,
            )
            for side, step, here, there in (
                (0, 1, has_above, has_below),
                (1, -1, has_below, has_above),
            )
        ]

    def later_copy(d, src, dst, send, recv, only=None):
        sends, receives = (t + d < slices, t >= d) if only is None else only
        return remote(src, dst, send, recv, {"tm": t + d}, sends, receives)

    always = (t >= 0, t >= 0)
    first_only = (leading, leading)

    def halo_copies(field, source, low_ring, high_ring, index, only):
        count = high_ring - low_ring + 1
        starts = (3 - high_ring, low_ring - 1)
        return beside_copies(
            (source.at[pl.ds(layers - high_ring, count)], source.at[pl.ds(low_ring - 1, count)]),
            lambda side: r.halo.at[field, side, pl.ds(starts[side], count)],
            r.halo_send.at[index],
            r.halo_recv.at[index],
            only=only,
        )

    guess_src, rate_src, control_src, init_src = sources
    near = halo_copies(0, guess_src, 1, 2, 0, always)
    near += halo_copies(1, rate_src, 1, 1, 1, always)
    near += halo_copies(2, control_src, 1, 1, 2, always)
    near += halo_copies(3, init_src, 1, 1, 3, first_only)
    far = halo_copies(1, rate_src, 2, 2, 4, always)
    far += halo_copies(0, guess_src, 3, 3, 5, always)
    far += halo_copies(2, control_src, 2, 2, 6, always)
    far += halo_copies(3, init_src, 2, 2, 7, first_only)

    lane = lax.broadcasted_iota(jnp.int32, (layers * rows, width), 1)
    lane3 = lax.broadcasted_iota(jnp.int32, (layers, rows, width), 2)
    row3 = lax.broadcasted_iota(jnp.int32, (layers, rows, width), 1)
    even_index = (2 * lane) % width
    odd_index = even_index + 1
    low_index = lane // 2
    high_index = low_index + width // 2

    def take(array, index):
        flat = array.reshape(-1, width)
        picked = jnp.take_along_axis(
            flat, index[: flat.shape[0]], axis=1, mode="promise_in_bounds"
        )
        return picked.reshape(array.shape)

    def split(low, high):
        front = lane3[: low.shape[0]] < width // 2
        return [
            jnp.where(front, take(low, index), take(high, index))
            for index in (even_index, odd_index)
        ]

    def core_of(field):
        for load in loads[field]:
            load.wait()
        out = []
        for px in range(2):
            low = r.raw[field, 0, :, pl.ds(px, rows, stride=2), :]
            high = r.raw[field, 1, :, pl.ds(px, rows, stride=2), :]
            out += split(low, high)
        return out

    def rim_of(field, ring):
        for side, index in ((0, 3 - ring), (1, ring - 1)):
            for half in range(2):
                r.rim[field, half, side, index] = r.halo[field, side, index, :, halves[half]]
        out = []
        for px in range(2):
            low, high = [
                jnp.concatenate(
                    [
                        r.rim[field, half, side, index, pl.ds(px, rows, stride=2), :][None]
                        for side, index in ((0, 3 - ring), (1, ring - 1))
                    ],
                    0,
                )
                for half in range(2)
            ]
            out += split(low, high)
        return out

    rim_side = lax.broadcasted_iota(jnp.int32, (2, rows, width), 0)
    rim_inside = ((rim_side == 0) & has_below) | ((rim_side == 1) & has_above)

    def inside(v):
        return jnp.where(rim_inside, v, 0.0)

    def down(v):
        return jnp.where(row3[: v.shape[0]] == 0, 0.0, pltpu.roll(v, 1, 1))

    def up(v):
        return jnp.where(row3[: v.shape[0]] == rows - 1, 0.0, pltpu.roll(v, rows - 1, 1))

    def right(v):
        return jnp.where(lane3[: v.shape[0]] == 0, 0.0, pltpu.roll(v, 1, 2))

    def left(v):
        return jnp.where(lane3[: v.shape[0]] == width - 1, 0.0, pltpu.roll(v, width - 1, 2))

    def planar(v):
        a, b, c, d = v
        return [
            (c + down(c)) + (b + right(b)),
            (d + down(d)) + (a + left(a)),
            (a + up(a)) + (d + right(d)),
            (b + up(b)) + (c + left(c)),
        ]

    def inner(v):
        below = jnp.concatenate([jnp.zeros_like(v[:1]), v[:-1]], 0)
        above = jnp.concatenate([v[1:], jnp.zeros_like(v[:1])], 0)
        return below + above

    def outer(rim):
        gap = jnp.zeros((layers - 2, rows, width), jnp.float32)
        return jnp.concatenate([rim[:1], gap, rim[1:]], 0)

    def ends_of(v):
        return jnp.concatenate([v[:1], v[layers - 1 :]], 0)

    def total(v):
        return (v[0] + v[1]) + (v[2] + v[3])

    def force_of(v, depth, control, rate):
        flat = planar(v)
        return [
            diffusion * (flat[p] + depth[p] - 6.0 * v[p])
            + jnp.tanh(v[p])
            + control[p]
            - rate[p] * v[p]
            for p in range(4)
        ]

    def sweep_of(start, integral, rate, nodes, inverse):
        return [
            [
                (start[p] + integral[m][p] + D[m] * rate[p] * nodes[m][p]) * inverse[m][p]
                for p in range(4)
            ]
            for m in range(3)
        ]

    def inverse_of(rate):
        return [[1.0 / (1.0 + D[m] * rate[p]) for p in range(4)] for m in range(3)]

    def scale_of(coarse_rate):
        return [1.0 / (1.0 + D[m] * coarse_rate) for m in range(3)]

    def first_sweep(start, force, rate, guess, inverse):
        integral = [[ROW[m] * force[p] for p in range(4)] for m in range(3)]
        return sweep_of(start, integral, rate, [guess] * 3, inverse)

    def mix(m, v):
        return Q[m][0] * v[0] + Q[m][1] * v[1] + Q[m][2] * v[2]

    guess = core_of(0)
    rate = core_of(1)
    coarse_rate = 0.25 * total(rate)
    scale = scale_of(coarse_rate)
    r.scale_buf[...] = scale[2]
    core_arrived, rim_arrived = [], []
    for d in range(1, slices):
        only = ((t > 0) & (t + d < slices), t > d)
        core_arrived.append(
            later_copy(
                d,
                r.scale_buf,
                r.scale_in.at[d - 1],
                r.scale_send.at[d - 1],
                r.scale_recv.at[d - 1],
                only,
            )
        )
        rim_arrived += beside_copies(
            (r.scale_buf.at[pl.ds(layers - 2, 2)], r.scale_buf.at[pl.ds(0, 2)]),
            lambda side: r.scale_rim_in.at[d - 1, side],
            r.scale_rim_send.at[d - 1],
            r.scale_rim_recv.at[d - 1],
            d,
            only,
        )
    control = core_of(2)
    initial = core_of(3)
    coarse_first = 0.25 * total(initial)
    coarse_control = 0.25 * total(control)
    start = [jnp.where(leading, initial[p], guess[p]) for p in range(4)]
    inverse = inverse_of(rate)

    force = force_of(guess, [inner(v) for v in guess], control, rate)
    for arrived in near:
        arrived()
    guess1, guess2 = rim_of(0, 1), rim_of(0, 2)
    rate1, control1, initial1 = rim_of(1, 1), rim_of(2, 1), rim_of(3, 1)
    force = [force[p] + diffusion * outer(guess1[p]) for p in range(4)]
    swept = first_sweep(start, force, rate, guess, inverse)
    inverse1 = inverse_of(rate1)
    start1 = [jnp.where(leading, initial1[p], guess1[p]) for p in range(4)]
    force1 = force_of(guess1, [guess2[p] + ends_of(guess[p]) for p in range(4)], control1, rate1)
    swept1 = first_sweep(start1, force1, rate1, guess1, inverse1)
    swept1 = [[inside(v) for v in node] for node in swept1]

    def offsets_of(swept, coarse, coarse_rim):
        restricted = []
        for j in range(3):
            a, b, c, d = swept[j]
            edges = (down(c + d) + up(a + b)) + (right(b + d) + left(a + c))
            local = [jnp.tanh(swept[j][p]) - rate[p] * swept[j][p] for p in range(4)]
            restricted.append(
                0.25 * (diffusion * edges + total(local))
                + diffusion * (inner(coarse[j]) - 4.0 * coarse[j] + outer(coarse_rim[j]))
                + coarse_control
            )
        return [
            scale[m] * (mix(m, restricted) + D[m] * coarse_rate * coarse[m]) for m in (0, 1, 2)
        ]

    def send_offset(it, last):
        r.offset_buf[it] = jnp.where(leading, scale[2] * coarse_first + last, last)
        return [
            later_copy(
                d,
                r.offset_buf.at[it],
                r.offset_in.at[it, d - 1],
                r.offset_send.at[it, d - 1],
                r.offset_recv.at[it, d - 1],
            )
            for d in reversed(range(1, slices))
        ]

    def chain(first, scales, offsets):
        current = first
        for d in reversed(range(1, slices)):
            moved = scales(d) * current + offsets(d)
            current = jnp.where(t > d, moved, jnp.where(t == d, offsets(d), current))
        return current

    coarse = [0.25 * total(swept[m]) for m in range(3)]
    coarse1 = [0.25 * total(swept1[m]) for m in range(3)]
    offset = offsets_of(swept, coarse, coarse1)
    core_arrived += send_offset(0, offset[2])
    for d in range(1, slices):
        rim_arrived += beside_copies(
            (r.offset_buf.at[0, pl.ds(layers - 2, 2)], r.offset_buf.at[0, pl.ds(0, 2)]),
            lambda side: r.offset_rim_in.at[d - 1, side],
            r.offset_rim_send.at[d - 1],
            r.offset_rim_recv.at[d - 1],
            d,
        )
    for m in range(3):
        r.own_buf[:, m] = offset[m]
    own_arrived = beside_copies(
        (r.own_buf.at[pl.ds(layers - 2, 2)], r.own_buf.at[pl.ds(0, 2)]),
        lambda side: r.own_rim.at[side],
        r.own_send,
        r.own_recv,
    )
    for p in range(4):
        r.end_buf[pl.ds(1, layers), p] = swept[2][p]
        r.end_buf[0, p] = swept1[2][p][0]
        r.end_buf[layers + 1, p] = swept1[2][p][1]
    end_arrived = later_copy(1, r.end_buf, r.end_in, r.end_send, r.end_recv)

    for arrived in far:
        arrived()
    guess3 = rim_of(0, 3)
    rate2, control2, initial2 = rim_of(1, 2), rim_of(2, 2), rim_of(3, 2)
    start2 = [jnp.where(leading, initial2[p], guess2[p]) for p in range(4)]
    force2 = force_of(guess2, [guess3[p] + guess1[p] for p in range(4)], control2, rate2)
    swept2 = first_sweep(start2, force2, rate2, guess2, inverse_of(rate2))
    coarse2 = [0.25 * total(swept2[m]) for m in range(3)]
    scale1, scale2 = scale_of(0.25 * total(rate1)), scale_of(0.25 * total(rate2))

    for arrived in core_arrived:
        arrived()
    coarse_start = chain(
        coarse_first, lambda d: r.scale_in[d - 1], lambda d: r.offset_in[0, d - 1]
    )

    correction = [scale[m] * coarse_start + offset[m] - coarse[m] for m in range(3)]
    nodes = [[swept[m][p] + correction[m] for p in range(4)] for m in range(3)]
    forces = [
        force_of(nodes[j], [inner(nodes[j][p]) for p in range(4)], control, rate)
        for j in range(3)
    ]
    for arrived in rim_arrived + own_arrived:
        arrived()

    def ring(ref, k):
        return jnp.concatenate([ref[0, 2 - k][None], ref[1, k - 1][None]], 0)

    start_rim = [
        chain(
            0.25 * total(initial_ring),
            lambda d: ring(r.scale_rim_in.at[d - 1], k),
            lambda d: ring(r.offset_rim_in.at[d - 1], k),
        )
        for k, initial_ring in ((1, initial1), (2, initial2))
    ]

    def rim_nodes(k, scales, coarses, sweeps):
        own = ring(r.own_rim, k)
        out = []
        for m in range(3):
            corrected = scales[m] * start_rim[k - 1] + own[:, m] - coarses[m]
            out.append([inside(sweeps[m][p] + corrected) for p in range(4)])
        return out

    nodes1 = rim_nodes(1, scale1, coarse1, swept1)
    nodes2 = rim_nodes(2, scale2, coarse2, swept2)
    forces = [
        [forces[j][p] + diffusion * outer(nodes1[j][p]) for p in range(4)] for j in range(3)
    ]
    forces1 = [
        force_of(
            nodes1[j],
            [nodes2[j][p] + ends_of(nodes[j][p]) for p in range(4)],
            control1,
            rate1,
        )
        for j in range(3)
    ]
    integral = [[mix(m, [forces[j][p] for j in range(3)]) for p in range(4)] for m in range(3)]
    integral1 = [[mix(m, [forces1[j][p] for j in range(3)]) for p in range(4)] for m in range(3)]
    end_arrived()
    ends = [r.end_in[pl.ds(1, layers), p] for p in range(4)]
    ends1 = [
        jnp.concatenate([r.end_in[0, p][None], r.end_in[layers + 1, p][None]], 0) for p in range(4)
    ]
    shift = coarse_start - 0.25 * total(ends)
    shift1 = start_rim[0] - 0.25 * total(ends1)
    start = [jnp.where(leading, initial[p], ends[p] + shift) for p in range(4)]
    start1 = [jnp.where(leading, initial1[p], ends1[p] + shift1) for p in range(4)]
    swept = sweep_of(start, integral, rate, nodes, inverse)
    swept1 = sweep_of(start1, integral1, rate1, nodes1, inverse1)

    coarse = [0.25 * total(swept[m]) for m in range(3)]
    coarse1 = [inside(0.25 * total(swept1[m])) for m in range(3)]
    offset = offsets_of(swept, coarse, coarse1)
    for arrived in send_offset(1, offset[2]):
        arrived()
    coarse_start = chain(
        coarse_first, lambda d: r.scale_in[d - 1], lambda d: r.offset_in[1, d - 1]
    )
    correction = [scale[m] * coarse_start + offset[m] - coarse[m] for m in range(3)]

    even_lane = lane3 % 2 == 0
    stores = []
    for m in range(3):
        node = [swept[m][p] + correction[m] for p in range(4)]
        for half, index in enumerate((low_index, high_index)):
            for px in range(2):
                r.out_buf[m, half, :, pl.ds(px, rows, stride=2), :] = jnp.where(
                    even_lane, take(node[2 * px], index), take(node[2 * px + 1], index)
                )
            store = pltpu.make_async_copy(
                r.out_buf.at[m, half],
                out_ref.at[0, m, :, :, halves[half]],
                r.out_sem.at[m, half],
            )
            store.start()
            stores.append(store)
    for sent in pending:
        sent()
    for store in stores:
        store.wait()


def per_device(initial_state, start_guess, control, reaction_rate):
    slices = lax.axis_size("tm")
    slabs = lax.axis_size("gz")
    layers, depth_rows, columns = initial_state.shape
    rows, width = depth_rows // 2, columns // 2
    later = slices - 1
    vmem = functools.partial(pltpu.VMEM, dtype=jnp.float32)
    dma = pltpu.SemaphoreType.DMA
    coarse = (layers, rows, width)
    scratch = dict(
        raw=vmem((4, 2, layers, depth_rows, width)),
        halo=vmem((4, 2, 3, depth_rows, columns)),
        rim=vmem((4, 2, 2, 3, depth_rows, width)),
        scale_buf=vmem(coarse),
        scale_in=vmem((later,) + coarse),
        scale_rim_in=vmem((later, 2, 2, rows, width)),
        offset_buf=vmem((ITERS,) + coarse),
        offset_in=vmem((ITERS, later) + coarse),
        offset_rim_in=vmem((later, 2, 2, rows, width)),
        own_buf=vmem((layers, 3, rows, width)),
        own_rim=vmem((2, 2, 3, rows, width)),
        end_buf=vmem((layers + 2, 4, rows, width)),
        end_in=vmem((layers + 2, 4, rows, width)),
        out_buf=vmem((3, 2, layers, depth_rows, width)),
        in_sem=dma((4, 2)),
        out_sem=dma((3, 2)),
        halo_send=dma((8, 2)),
        halo_recv=dma((8, 2)),
        scale_send=dma((later,)),
        scale_recv=dma((later,)),
        scale_rim_send=dma((later, 2)),
        scale_rim_recv=dma((later, 2)),
        offset_send=dma((ITERS, later)),
        offset_recv=dma((ITERS, later)),
        offset_rim_send=dma((later, 2)),
        offset_rim_recv=dma((later, 2)),
        own_send=dma((2,)),
        own_recv=dma((2,)),
        end_send=dma,
        end_recv=dma,
    )
    names = list(scratch)

    def body(*refs):
        kernel(slices, slabs, *refs[:5], types.SimpleNamespace(**dict(zip(names, refs[5:]))))

    return pl.pallas_call(
        body,
        out_shape=jax.ShapeDtypeStruct((1, 3, layers, depth_rows, columns), jnp.float32),
        in_specs=[pl.BlockSpec(memory_space=pl.ANY)] * 4,
        out_specs=pl.BlockSpec(memory_space=pl.ANY),
        scratch_shapes=list(scratch.values()),
        compiler_params=pltpu.CompilerParams(
            collective_id=0, has_side_effects=True, vmem_limit_bytes=VMEM_LIMIT
        ),
    )(initial_state, start_guess, control, reaction_rate)


def solution(mesh):
    in_specs = (
        P(("groups", "gz"), None, None),
        P("tm", ("groups", "gz"), None, None),
        P("tm", ("groups", "gz"), None, None),
        P("tm", ("groups", "gz"), None, None),
    )
    out_specs = P("tm", None, ("groups", "gz"), None, None)
    return jax.shard_map(
        per_device, mesh=mesh, in_specs=in_specs, out_specs=out_specs, check_vma=False
    )
```

```python
import functools
import math
import types

import jax
import jax.numpy as jnp
from jax import lax
from jax.experimental import pallas as pl
from jax.experimental.pallas import tpu as pltpu
from jax.sharding import PartitionSpec as P

ITERS = 2

root_six = math.sqrt(6.0)
Q = (
    (
        (88.0 - 7.0 * root_six) / 360.0,
        (296.0 - 169.0 * root_six) / 1800.0,
        (-2.0 + 3.0 * root_six) / 225.0,
    ),
    (
        (296.0 + 169.0 * root_six) / 1800.0,
        (88.0 + 7.0 * root_six) / 360.0,
        (-2.0 - 3.0 * root_six) / 225.0,
    ),
    ((16.0 - root_six) / 36.0, (16.0 + root_six) / 36.0, 1.0 / 9.0),
)
D = tuple(Q[m][m] for m in range(3))
ROW = tuple(sum(Q[m]) for m in range(3))
diffusion = 0.1
VMEM_LIMIT = 60 * 1024 * 1024
MESH = pl.DeviceIdType.MESH


def kernel(slices, slabs, init_ref, guess_ref, control_ref, rate_ref, out_ref, r):
    t = lax.axis_index("tm")
    z = lax.axis_index("gz")
    layers, depth_rows, width = r.raw.shape[2:]
    rows = depth_rows // 2
    has_above = z < slabs - 1
    has_below = z > 0
    leading = t == 0

    sources = (guess_ref.at[0], rate_ref.at[0], control_ref.at[0], init_ref)
    halves = [pl.ds(half * width, width) for half in range(2)]
    loads = [
        [
            pltpu.make_async_copy(
                source.at[:, :, halves[half]], r.raw.at[field, half], r.in_sem.at[field, half]
            )
            for half in range(2)
        ]
        for field, source in enumerate(sources)
    ]
    for pair in loads:
        for load in pair:
            load.start()

    barrier = pltpu.get_barrier_semaphore()

    def greet(condition, device):
        @pl.when(condition)
        def _():
            pl.semaphore_signal(barrier, inc=1, device_id=device, device_id_type=MESH)

    greet(has_above, {"gz": z + 1})
    greet(has_below, {"gz": z - 1})
    for d in range(1, slices):
        greet(t >= d, {"tm": t - d})
    beside = has_above.astype(jnp.int32) + has_below.astype(jnp.int32)

    @pl.when(z == 0)
    def _():
        r.halo[:, 0] = jnp.zeros_like(r.halo[:, 0])

    @pl.when(z == slabs - 1)
    def _():
        r.halo[:, 1] = jnp.zeros_like(r.halo[:, 1])

    pl.semaphore_wait(barrier, beside + (slices - 1 - t))

    pending = []

    def remote(src, dst, send, recv, device, sends, receives):
        copy = pltpu.make_async_remote_copy(
            src_ref=src,
            dst_ref=dst,
            send_sem=send,
            recv_sem=recv,
            device_id=device,
            device_id_type=MESH,
        )

        @pl.when(sends)
        def _():
            copy.start()

        def sent():
            @pl.when(sends)
            def _():
                copy.wait_send()

        def arrived():
            @pl.when(receives)
            def _():
                copy.wait_recv()

        pending.append(sent)
        return arrived

    def beside_copies(sources, dst, send, recv, d=0, only=None):
        sends = t + d < slices
        receives = t >= d
        if only is not None:
            sends, receives = only
        return [
            remote(
                sources[side],
                dst(side),
                send.at[side],
                recv.at[side],
                {"tm": t + d, "gz": z + step},
                sends & here,
                receives & there,
            )
            for side, step, here, there in (
                (0, 1, has_above, has_below),
                (1, -1, has_below, has_above),
            )
        ]

    def later_copy(d, src, dst, send, recv, only=None):
        sends, receives = (t + d < slices, t >= d) if only is None else only
        return remote(src, dst, send, recv, {"tm": t + d}, sends, receives)

    always = (t >= 0, t >= 0)
    first_only = (leading, leading)

    def halo_copies(field, source, low_ring, high_ring, index, only):
        count = high_ring - low_ring + 1
        starts = (4 - high_ring, low_ring - 1)
        return beside_copies(
            (source.at[pl.ds(layers - high_ring, count)], source.at[pl.ds(low_ring - 1, count)]),
            lambda side: r.halo.at[field, side, pl.ds(starts[side], count)],
            r.halo_send.at[index],
            r.halo_recv.at[index],
            only=only,
        )

    guess_src, rate_src, control_src, init_src = sources
    near = halo_copies(0, guess_src, 1, 2, 0, always)
    near += halo_copies(1, rate_src, 1, 1, 1, always)
    near += halo_copies(2, control_src, 1, 1, 2, always)
    near += halo_copies(3, init_src, 1, 1, 3, first_only)
    far = halo_copies(1, rate_src, 2, 3, 4, always)
    far += halo_copies(0, guess_src, 3, 4, 5, always)
    far += halo_copies(2, control_src, 2, 3, 6, always)
    far += halo_copies(3, init_src, 2, 3, 7, first_only)

    lane = lax.broadcasted_iota(jnp.int32, (layers * rows, width), 1)
    lane3 = lax.broadcasted_iota(jnp.int32, (layers, rows, width), 2)
    row3 = lax.broadcasted_iota(jnp.int32, (layers, rows, width), 1)
    even_index = (2 * lane) % width
    odd_index = even_index + 1
    low_index = lane // 2
    high_index = low_index + width // 2

    def take(array, index):
        flat = array.reshape(-1, width)
        picked = jnp.take_along_axis(
            flat, index[: flat.shape[0]], axis=1, mode="promise_in_bounds"
        )
        return picked.reshape(array.shape)

    def split(low, high):
        front = lane3[: low.shape[0]] < width // 2
        return [
            jnp.where(front, take(low, index), take(high, index))
            for index in (even_index, odd_index)
        ]

    def core_of(field):
        for load in loads[field]:
            load.wait()
        out = []
        for px in range(2):
            low = r.raw[field, 0, :, pl.ds(px, rows, stride=2), :]
            high = r.raw[field, 1, :, pl.ds(px, rows, stride=2), :]
            out += split(low, high)
        return out

    def rim_of(field, ring):
        for side, index in ((0, 4 - ring), (1, ring - 1)):
            for half in range(2):
                r.rim[field, half, side, index] = r.halo[field, side, index, :, halves[half]]
        out = []
        for px in range(2):
            low, high = [
                jnp.concatenate(
                    [
                        r.rim[field, half, side, index, pl.ds(px, rows, stride=2), :][None]
                        for side, index in ((0, 4 - ring), (1, ring - 1))
                    ],
                    0,
                )
                for half in range(2)
            ]
            out += split(low, high)
        return out

    rim_side = lax.broadcasted_iota(jnp.int32, (2, rows, width), 0)
    rim_inside = ((rim_side == 0) & has_below) | ((rim_side == 1) & has_above)

    def inside(v):
        return jnp.where(rim_inside, v, 0.0)

    def down(v):
        return jnp.where(row3[: v.shape[0]] == 0, 0.0, pltpu.roll(v, 1, 1))

    def up(v):
        return jnp.where(row3[: v.shape[0]] == rows - 1, 0.0, pltpu.roll(v, rows - 1, 1))

    def right(v):
        return jnp.where(lane3[: v.shape[0]] == 0, 0.0, pltpu.roll(v, 1, 2))

    def left(v):
        return jnp.where(lane3[: v.shape[0]] == width - 1, 0.0, pltpu.roll(v, width - 1, 2))

    def planar(v):
        a, b, c, d = v
        return [
            (c + down(c)) + (b + right(b)),
            (d + down(d)) + (a + left(a)),
            (a + up(a)) + (d + right(d)),
            (b + up(b)) + (c + left(c)),
        ]

    def inner(v):
        below = jnp.concatenate([jnp.zeros_like(v[:1]), v[:-1]], 0)
        above = jnp.concatenate([v[1:], jnp.zeros_like(v[:1])], 0)
        return below + above

    def outer(rim):
        gap = jnp.zeros((layers - 2, rows, width), jnp.float32)
        return jnp.concatenate([rim[:1], gap, rim[1:]], 0)

    def ends_of(v):
        return jnp.concatenate([v[:1], v[layers - 1 :]], 0)

    def total(v):
        return (v[0] + v[1]) + (v[2] + v[3])

    def force_of(v, depth, control, rate):
        flat = planar(v)
        return [
            diffusion * (flat[p] + depth[p] - 6.0 * v[p])
            + jnp.tanh(v[p])
            + control[p]
            - rate[p] * v[p]
            for p in range(4)
        ]

    def sweep_of(start, integral, rate, nodes, inverse):
        return [
            [
                (start[p] + integral[m][p] + D[m] * rate[p] * nodes[m][p]) * inverse[m][p]
                for p in range(4)
            ]
            for m in range(3)
        ]

    def inverse_of(rate):
        return [[1.0 / (1.0 + D[m] * rate[p]) for p in range(4)] for m in range(3)]

    def scale_of(coarse_rate):
        return [1.0 / (1.0 + D[m] * coarse_rate) for m in range(3)]

    def first_sweep(start, force, rate, guess, inverse):
        integral = [[ROW[m] * force[p] for p in range(4)] for m in range(3)]
        return sweep_of(start, integral, rate, [guess] * 3, inverse)

    def mix(m, v):
        return Q[m][0] * v[0] + Q[m][1] * v[1] + Q[m][2] * v[2]

    guess = core_of(0)
    rate = core_of(1)
    coarse_rate = 0.25 * total(rate)
    scale = scale_of(coarse_rate)
    r.scale_buf[...] = scale[2]
    core_arrived, rim_arrived = [], []
    for d in range(1, slices):
        only = ((t > 0) & (t + d < slices), t > d)
        core_arrived.append(
            later_copy(
                d,
                r.scale_buf,
                r.scale_in.at[d - 1],
                r.scale_send.at[d - 1],
                r.scale_recv.at[d - 1],
                only,
            )
        )
    control = core_of(2)
    initial = core_of(3)
    coarse_first = 0.25 * total(initial)
    coarse_control = 0.25 * total(control)
    start = [jnp.where(leading, initial[p], guess[p]) for p in range(4)]
    inverse = inverse_of(rate)

    force = force_of(guess, [inner(v) for v in guess], control, rate)
    for arrived in near:
        arrived()
    guess1, guess2 = rim_of(0, 1), rim_of(0, 2)
    rate1, control1, initial1 = rim_of(1, 1), rim_of(2, 1), rim_of(3, 1)
    force = [force[p] + diffusion * outer(guess1[p]) for p in range(4)]
    swept = first_sweep(start, force, rate, guess, inverse)
    inverse1 = inverse_of(rate1)
    start1 = [jnp.where(leading, initial1[p], guess1[p]) for p in range(4)]
    force1 = force_of(guess1, [guess2[p] + ends_of(guess[p]) for p in range(4)], control1, rate1)
    swept1 = first_sweep(start1, force1, rate1, guess1, inverse1)
    swept1 = [[inside(v) for v in node] for node in swept1]

    def offsets_of(swept, coarse, depth, coarse_control, rate, coarse_rate, scale):
        restricted = []
        for j in range(3):
            a, b, c, d = swept[j]
            edges = (down(c + d) + up(a + b)) + (right(b + d) + left(a + c))
            local = [jnp.tanh(swept[j][p]) - rate[p] * swept[j][p] for p in range(4)]
            restricted.append(
                0.25 * (diffusion * edges + total(local))
                + diffusion * (depth[j] - 4.0 * coarse[j])
                + coarse_control
            )
        return [
            scale[m] * (mix(m, restricted) + D[m] * coarse_rate * coarse[m]) for m in (0, 1, 2)
        ]

    def send_offset(it, last):
        r.offset_buf[it] = jnp.where(leading, scale[2] * coarse_first + last, last)
        return [
            later_copy(
                d,
                r.offset_buf.at[it],
                r.offset_in.at[it, d - 1],
                r.offset_send.at[it, d - 1],
                r.offset_recv.at[it, d - 1],
            )
            for d in reversed(range(1, slices))
        ]

    def chain(first, scales, offsets):
        current = first
        for d in reversed(range(1, slices)):
            moved = scales(d) * current + offsets(d)
            current = jnp.where(t > d, moved, jnp.where(t == d, offsets(d), current))
        return current

    coarse = [0.25 * total(swept[m]) for m in range(3)]
    coarse1 = [0.25 * total(swept1[m]) for m in range(3)]
    depth = [inner(coarse[j]) + outer(coarse1[j]) for j in range(3)]
    offset = offsets_of(swept, coarse, depth, coarse_control, rate, coarse_rate, scale)
    core_arrived += send_offset(0, offset[2])
    for p in range(4):
        r.end_buf[pl.ds(1, layers), p] = swept[2][p]
        r.end_buf[0, p] = swept1[2][p][0]
        r.end_buf[layers + 1, p] = swept1[2][p][1]

    for arrived in far:
        arrived()
    guess3, guess4 = rim_of(0, 3), rim_of(0, 4)
    rate2, control2, initial2 = rim_of(1, 2), rim_of(2, 2), rim_of(3, 2)
    rate3, control3, initial3 = rim_of(1, 3), rim_of(2, 3), rim_of(3, 3)
    start2 = [jnp.where(leading, initial2[p], guess2[p]) for p in range(4)]
    force2 = force_of(guess2, [guess3[p] + guess1[p] for p in range(4)], control2, rate2)
    swept2 = first_sweep(start2, force2, rate2, guess2, inverse_of(rate2))
    coarse2 = [0.25 * total(swept2[m]) for m in range(3)]
    start3 = [jnp.where(leading, initial3[p], guess3[p]) for p in range(4)]
    force3 = force_of(guess3, [guess4[p] + guess2[p] for p in range(4)], control3, rate3)
    swept3 = first_sweep(start3, force3, rate3, guess3, inverse_of(rate3))
    coarse2 = [inside(v) for v in coarse2]
    coarse3 = [inside(0.25 * total(swept3[m])) for m in range(3)]
    coarse_rate1, coarse_rate2 = 0.25 * total(rate1), 0.25 * total(rate2)
    scale1, scale2 = scale_of(coarse_rate1), scale_of(coarse_rate2)
    offset1 = offsets_of(
        swept1,
        coarse1,
        [coarse2[j] + ends_of(coarse[j]) for j in range(3)],
        0.25 * total(control1),
        rate1,
        coarse_rate1,
        scale1,
    )
    offset2 = offsets_of(
        swept2,
        coarse2,
        [coarse3[j] + coarse1[j] for j in range(3)],
        0.25 * total(control2),
        rate2,
        coarse_rate2,
        scale2,
    )
    first1, first2 = 0.25 * total(initial1), 0.25 * total(initial2)
    for k, first, scales, last in ((0, first1, scale1[2], offset1[2]), (1, first2, scale2[2], offset2[2])):
        r.rim_buf[0, k] = scales
        r.rim_buf[1, k] = jnp.where(leading, scales * first + last, last)
    for d in reversed(range(1, slices)):
        rim_arrived.append(
            later_copy(
                d, r.rim_buf, r.rim_in.at[d - 1], r.rim_send.at[d - 1], r.rim_recv.at[d - 1]
            )
        )
    end_arrived = later_copy(1, r.end_buf, r.end_in, r.end_send, r.end_recv)

    for arrived in core_arrived:
        arrived()
    coarse_start = chain(
        coarse_first, lambda d: r.scale_in[d - 1], lambda d: r.offset_in[0, d - 1]
    )

    correction = [scale[m] * coarse_start + offset[m] - coarse[m] for m in range(3)]
    nodes = [[swept[m][p] + correction[m] for p in range(4)] for m in range(3)]
    forces = [
        force_of(nodes[j], [inner(nodes[j][p]) for p in range(4)], control, rate)
        for j in range(3)
    ]
    for arrived in rim_arrived:
        arrived()

    start_rim = [
        chain(first, lambda d: r.rim_in[d - 1, 0, k], lambda d: r.rim_in[d - 1, 1, k])
        for k, first in ((0, first1), (1, first2))
    ]

    def rim_nodes(k, scales, offsets, coarses, sweeps):
        out = []
        for m in range(3):
            corrected = scales[m] * start_rim[k - 1] + offsets[m] - coarses[m]
            out.append([inside(sweeps[m][p] + corrected) for p in range(4)])
        return out

    nodes1 = rim_nodes(1, scale1, offset1, coarse1, swept1)
    nodes2 = rim_nodes(2, scale2, offset2, coarse2, swept2)
    forces = [
        [forces[j][p] + diffusion * outer(nodes1[j][p]) for p in range(4)] for j in range(3)
    ]
    forces1 = [
        force_of(
            nodes1[j],
            [nodes2[j][p] + ends_of(nodes[j][p]) for p in range(4)],
            control1,
            rate1,
        )
        for j in range(3)
    ]
    integral = [[mix(m, [forces[j][p] for j in range(3)]) for p in range(4)] for m in range(3)]
    integral1 = [[mix(m, [forces1[j][p] for j in range(3)]) for p in range(4)] for m in range(3)]
    end_arrived()
    ends = [r.end_in[pl.ds(1, layers), p] for p in range(4)]
    ends1 = [
        jnp.concatenate([r.end_in[0, p][None], r.end_in[layers + 1, p][None]], 0) for p in range(4)
    ]
    shift = coarse_start - 0.25 * total(ends)
    shift1 = start_rim[0] - 0.25 * total(ends1)
    start = [jnp.where(leading, initial[p], ends[p] + shift) for p in range(4)]
    start1 = [jnp.where(leading, initial1[p], ends1[p] + shift1) for p in range(4)]
    swept = sweep_of(start, integral, rate, nodes, inverse)
    swept1 = sweep_of(start1, integral1, rate1, nodes1, inverse1)

    coarse = [0.25 * total(swept[m]) for m in range(3)]
    coarse1 = [inside(0.25 * total(swept1[m])) for m in range(3)]
    depth = [inner(coarse[j]) + outer(coarse1[j]) for j in range(3)]
    offset = offsets_of(swept, coarse, depth, coarse_control, rate, coarse_rate, scale)
    for arrived in send_offset(1, offset[2]):
        arrived()
    coarse_start = chain(
        coarse_first, lambda d: r.scale_in[d - 1], lambda d: r.offset_in[1, d - 1]
    )
    correction = [scale[m] * coarse_start + offset[m] - coarse[m] for m in range(3)]

    even_lane = lane3 % 2 == 0
    stores = []
    for m in range(3):
        node = [swept[m][p] + correction[m] for p in range(4)]
        for half, index in enumerate((low_index, high_index)):
            for px in range(2):
                r.out_buf[m, half, :, pl.ds(px, rows, stride=2), :] = jnp.where(
                    even_lane, take(node[2 * px], index), take(node[2 * px + 1], index)
                )
            store = pltpu.make_async_copy(
                r.out_buf.at[m, half],
                out_ref.at[0, m, :, :, halves[half]],
                r.out_sem.at[m, half],
            )
            store.start()
            stores.append(store)
    for sent in pending:
        sent()
    for store in stores:
        store.wait()


def per_device(initial_state, start_guess, control, reaction_rate):
    slices = lax.axis_size("tm")
    slabs = lax.axis_size("gz")
    layers, depth_rows, columns = initial_state.shape
    rows, width = depth_rows // 2, columns // 2
    later = slices - 1
    vmem = functools.partial(pltpu.VMEM, dtype=jnp.float32)
    dma = pltpu.SemaphoreType.DMA
    coarse = (layers, rows, width)
    scratch = dict(
        raw=vmem((4, 2, layers, depth_rows, width)),
        halo=vmem((4, 2, 4, depth_rows, columns)),
        rim=vmem((4, 2, 2, 4, depth_rows, width)),
        scale_buf=vmem(coarse),
        scale_in=vmem((later,) + coarse),
        offset_buf=vmem((ITERS,) + coarse),
        offset_in=vmem((ITERS, later) + coarse),
        rim_buf=vmem((2, 2, 2, rows, width)),
        rim_in=vmem((later, 2, 2, 2, rows, width)),
        end_buf=vmem((layers + 2, 4, rows, width)),
        end_in=vmem((layers + 2, 4, rows, width)),
        out_buf=vmem((3, 2, layers, depth_rows, width)),
        in_sem=dma((4, 2)),
        out_sem=dma((3, 2)),
        halo_send=dma((8, 2)),
        halo_recv=dma((8, 2)),
        scale_send=dma((later,)),
        scale_recv=dma((later,)),
        offset_send=dma((ITERS, later)),
        offset_recv=dma((ITERS, later)),
        rim_send=dma((later,)),
        rim_recv=dma((later,)),
        end_send=dma,
        end_recv=dma,
    )
    names = list(scratch)

    def body(*refs):
        kernel(slices, slabs, *refs[:5], types.SimpleNamespace(**dict(zip(names, refs[5:]))))

    return pl.pallas_call(
        body,
        out_shape=jax.ShapeDtypeStruct((1, 3, layers, depth_rows, columns), jnp.float32),
        in_specs=[pl.BlockSpec(memory_space=pl.ANY)] * 4,
        out_specs=pl.BlockSpec(memory_space=pl.ANY),
        scratch_shapes=list(scratch.values()),
        compiler_params=pltpu.CompilerParams(
            collective_id=0, has_side_effects=True, vmem_limit_bytes=VMEM_LIMIT
        ),
    )(initial_state, start_guess, control, reaction_rate)


def solution(mesh):
    in_specs = (
        P(("groups", "gz"), None, None),
        P("tm", ("groups", "gz"), None, None),
        P("tm", ("groups", "gz"), None, None),
        P("tm", ("groups", "gz"), None, None),
    )
    out_specs = P("tm", None, ("groups", "gz"), None, None)
    return jax.shard_map(
        per_device, mesh=mesh, in_specs=in_specs, out_specs=out_specs, check_vma=False
    )
```
